32 devices in a mesh: prow: 4 (over y, core), pcol: 8 (over z, x).
Axes of the slice: x: 2, y: 2, z: 4, core: 2. Of those that a mesh axis runs over, the one named last changes fastest.
Arguments:
- diag_one: float32 [1024, 1024], P('pcol')
- top_rows: bfloat16 [1024, 1024], P('pcol'), may hold values from -0.1875 to 0.1875
- panel_one: bfloat16 [16384, 1024], P(('prow', 'pcol')), may hold values from -6 to 6
- first_block: int32 [64], P(('prow', 'pcol')), may hold values from 0 to 3
- target: int32 [64], P(('prow', 'pcol')), may hold values from 0 to 63, as said below
- diag_two: float32 [1024, 1024], P('pcol'), may hold values from -6 to 6
- panel_two: bfloat16 [16384, 1024], P(('prow', 'pcol')), may hold values from -6 to 6
Outputs:
- panel_factor: bfloat16 [16384, 1024], P(('prow', 'pcol'))
- top_factor: bfloat16 [1024, 1024], P('pcol')
- diag_next: float32 [1024, 1024], P('pcol')
- panel_next: float32 [16384, 1024], P(('prow', 'pcol'))
The draws below stay inside these ranges and needn't reach their ends.
Inputs may be any that keep to these rules, and one draw needn't show every extreme that they name: Row block t of the second supernode is held by grid row (t // 2) // 8 and grid column (t // 2) % 8; target[i] lies in the grid column of row block i; the 2 row blocks of one device go to 2 different grid rows; in every grid column one grid row receives a row block from every grid row.
All inputs are finite; a program needn't handle non-finite values.
Results may differ from the reference program's by a relative error of at most 0.0021.
Values may be sent and summed in bfloat16 or wider, within the bound.
No kernel may reach another device: no remote copies, remote signals or barrier semaphores. Data moves between devices by JAX's collectives and lax.ppermute only.
A program may use at most 128 MiB of HBM per device.

```python
import math
import jax
import jax.numpy as jnp
from jax import lax

W = 1024
B = 256
RB_DEV = 2
NRB = 64
N_PROW = 4
N_PCOL = 8
DEVICES = 32


def draw_diag_one(key, part):
    key_off, key_diag = jax.random.split(key, 2)
    noise = jax.random.uniform(key_off, (W, W), jnp.float32, -1.0, 1.0)
    index = jnp.arange(W)
    coupling_scale = 0.96 / math.sqrt(W)
    coupled = 0.5 * (noise + noise.T) * coupling_scale
    coupled = jnp.where(index[:, None] != index[None, :], coupled, 0.0)
    diagonal = 1.5 + jax.random.uniform(key_diag, (W,), jnp.float32)
    return (coupled + jnp.diag(diagonal)).astype(jnp.float32)


def draw_target(key, part):
    key_hot, key_order, key_turn, key_slot = jax.random.split(key, 4)
    hot_row = jax.random.randint(key_hot, (N_PCOL,), 0, N_PROW)
    device = jnp.arange(DEVICES)
    grid_col = device % N_PCOL
    hot_each = hot_row[grid_col]
    scores = jax.random.randint(key_order, (DEVICES, N_PROW - 1), 0, 1 << 20) * N_PROW + jnp.arange(N_PROW - 1)[None, :]
    order = jnp.argsort(scores, axis=1).astype(jnp.int32)
    offsets = jnp.concatenate([jnp.zeros((DEVICES, 1), jnp.int32), order + 1], axis=1)[:, :RB_DEV]
    turn = jax.random.randint(key_turn, (DEVICES,), 0, RB_DEV)
    picked = (jnp.arange(RB_DEV)[None, :] + turn[:, None]) % RB_DEV
    chosen = jnp.take_along_axis(offsets, picked, axis=1)
    dest_row = (hot_each[:, None] + chosen) % N_PROW
    slot = jax.random.randint(key_slot, (DEVICES, RB_DEV), 0, RB_DEV)
    result = (dest_row * N_PCOL + grid_col[:, None]) * RB_DEV + slot
    return result.reshape(-1).astype(jnp.int32)


def set_ends(entries, key, least, largest):
    shape = entries.shape
    place = [jax.random.randint(jax.random.fold_in(key, axis), (), 0, shape[axis]) for axis in range(len(shape))]
    entries = entries.at[tuple(place)].set(least)
    longest = shape.index(max(shape))
    place[longest] = (place[longest] + 1) % shape[longest]
    return entries.at[tuple(place)].set(largest)


def levels(stream_key, dims, cuts, least, top_value):
    gain, own = 1.0, jax.random.fold_in(stream_key, 6)
    for axis_at, parts in cuts:
        steps = jnp.exp(jax.random.uniform(jax.random.fold_in(own, axis_at), (parts,), jnp.float32, least / len(cuts), top_value / len(cuts)))
        gain = gain * jnp.repeat(steps, dims[axis_at] // parts).reshape([-1 if axis == axis_at else 1 for axis in range(len(dims))])
    return gain


def bell_draw(rng, shape, scale, limit, cuts=(), kind=jnp.bfloat16):
    factor_of = levels(rng, shape, cuts, -0.22, 0.18) if cuts else 1.0
    entries = jax.random.normal(rng, shape, jnp.float32) * scale * factor_of
    return jnp.minimum(jnp.maximum(entries, -limit), limit).astype(kind)


def setup_inputs(seed: int = 0) -> dict:
    keys = jax.random.split(jax.random.key(seed), 8)
    return {
        "diag_one": draw_diag_one(jax.random.fold_in(keys[7], 71), 0),
        "top_rows": bell_draw(keys[1], (W, W), W ** -0.5, 0.1875, ((0, 8),)),
        "panel_one": bell_draw(keys[2], (NRB * B, W), 1.0, 6.0, ((0, 32),)),
        "first_block": set_ends(jax.random.randint(keys[3], (NRB,), 0, W // B), jax.random.fold_in(keys[3], 1), 0, (W // B) - 1).astype(jnp.int32),
        "target": draw_target(jax.random.fold_in(keys[7], 71), 0),
        "diag_two": bell_draw(keys[5], (W, W), 1.0, 6.0, ((0, 8),), jnp.float32),
        "panel_two": bell_draw(keys[6], (NRB * B, W), 1.0, 6.0, ((0, 32),)),
    }


def solve_rows(factor, operand):
    return lax.linalg.triangular_solve(factor, operand, left_side=False, lower=True, transpose_a=True)

def reference(diag_one, top_rows, panel_one, first_block, target, diag_two, panel_two):
    factor = jnp.linalg.cholesky(diag_one)
    top_factor = solve_rows(factor, top_rows.astype(jnp.float32)).astype(jnp.bfloat16)
    col_count = diag_one.shape[1]
    block_count = first_block.shape[0]
    col_block = jnp.arange(col_count, dtype=jnp.int32) // B
    stacked = panel_one.reshape(block_count, B, col_count)

    def one_block(item):
        block_in, first = item
        masked = jnp.where(col_block[None, :] >= first, block_in, jnp.zeros_like(block_in))
        solved = solve_rows(factor, masked.astype(jnp.float32)).astype(jnp.bfloat16)
        update = jnp.dot(solved.astype(jnp.float32), top_factor.T.astype(jnp.float32), preferred_element_type=jnp.float32).astype(jnp.bfloat16)
        return (solved, update)
    panel_blocks, update_blocks = lax.map(one_block, (stacked, first_block))
    widened = lax.optimization_barrier(update_blocks).astype(jnp.float32)
    summed = jax.ops.segment_sum(widened, target, num_segments=panel_two.shape[0] // B)
    panel_next = panel_two.astype(jnp.float32) - summed.reshape(-1, col_count)
    diag_next = diag_two - jnp.dot(top_factor.astype(jnp.float32), top_factor.T.astype(jnp.float32), preferred_element_type=jnp.float32)
    return (panel_blocks.reshape(-1, col_count), top_factor, diag_next, panel_next)
```

```python
import functools

import jax
import jax.numpy as jnp
from jax import lax
from jax.experimental import pallas as pl
from jax.experimental.pallas import tpu as pltpu
from jax.sharding import PartitionSpec as P

NB = 128
SUB = 32
VMEM = pl.BlockSpec(memory_space=pltpu.VMEM)


def split3(x):
    hi = x.astype(jnp.bfloat16)
    rest = x - hi.astype(jnp.float32)
    mid = rest.astype(jnp.bfloat16)
    low = (rest - mid.astype(jnp.float32)).astype(jnp.bfloat16)
    return hi, mid, low


def left_terms(x):
    hi, mid, low = split3(x)
    return jnp.concatenate([hi, hi, mid, hi, low, mid], 0)


def right_terms(x):
    hi, mid, low = split3(x)
    return jnp.concatenate([hi, mid, hi, low, hi, mid], 0)


def dot_tn(left, right):
    return lax.dot_general(
        left, right, (((0,), (0,)), ((), ())), preferred_element_type=jnp.float32
    )


def dot_nt(left, right):
    return lax.dot_general(
        left, right, (((1,), (1,)), ((), ())), preferred_element_type=jnp.float32
    )


def lanes(x, column, width):
    return jnp.broadcast_to(x[:, column : column + 1], (x.shape[0], width))


def wide(x, width):
    return jnp.tile(x, (1, width // x.shape[1]))


def eliminate(rows, base):
    width = rows[0].shape[1]
    groups = len(rows)
    rows = list(rows)
    done = []
    sublane = lax.broadcasted_iota(jnp.int32, (8, width), 0)
    for q in range(groups):
        first = base + 8 * q
        cols = [lanes(rows[q], first + c, NB) for c in range(8)]
        entry = {}
        for c in range(8):
            for i in range(c, 8):
                entry[i, c] = jnp.broadcast_to(cols[c][i : i + 1, :], (8, NB))
        row = [jnp.broadcast_to(rows[q][i : i + 1, :], (8, width)) for i in range(8)]
        below = [
            [lanes(rows[p], first + c, NB) for c in range(8)] for p in range(q + 1, groups)
        ]
        scale = []
        for j in range(8):
            pivot = entry[j, j]
            inverse = 1.0 / pivot
            scale.append(lax.rsqrt(pivot))
            ratio = {c: entry[c, j] * inverse for c in range(j + 1, 8)}
            for c in range(j + 1, 8):
                for i in range(c, 8):
                    entry[i, c] = entry[i, c] - entry[i, j] * ratio[c]
                row[c] = row[c] - wide(ratio[c], width) * row[j]
            for part in below:
                for c in range(j + 1, 8):
                    part[c] = part[c] - part[j] * ratio[c]
        final = [row[i] * wide(scale[i], width) for i in range(8)]
        merged = final[0]
        for i in range(1, 8):
            merged = jnp.where(sublane == i, final[i], merged)
        done.append(merged)
        for p, part in enumerate(below):
            for c in range(8):
                rows[q + 1 + p] = rows[q + 1 + p] - wide(part[c] * scale[c], width) * final[c]
    return done


def factor_block(block):
    rows = [block[8 * i : 8 * i + 8] for i in range(NB // 8)]
    step = SUB // 8
    done = []
    for b in range(NB // SUB):
        part = eliminate(rows[b * step : (b + 1) * step], b * SUB)
        done += part
        if (b + 1) * SUB < NB:
            solved = jnp.concatenate(part, 0)
            change = dot_tn(left_terms(solved[:, (b + 1) * SUB : NB]), right_terms(solved))
            for p in range((b + 1) * step, NB // 8):
                k = p - (b + 1) * step
                rows[p] = rows[p] - change[8 * k : 8 * k + 8]
    return jnp.concatenate(done, 0)


def factor_kernel(diag_ref, hi_ref, lo_ref, work, block, left, right):
    size = diag_ref.shape[0]
    count = size // NB
    work[...] = diag_ref[...]
    same = lax.broadcasted_iota(jnp.int32, (NB, NB), 0) == lax.broadcasted_iota(
        jnp.int32, (NB, NB), 1
    )
    unit = same.astype(jnp.float32)

    def step(k, carry):
        here = pl.ds(pl.multiple_of(k * NB, NB), NB)
        block[:, :NB] = work[here, here]
        block[:, NB:] = unit
        block[...] = factor_block(block[...])
        inverse = block[:, NB:]
        solved = dot_tn(left_terms(inverse.T), right_terms(work[here, :]))
        work[here, :] = solved
        work[here, here] = inverse
        solved = work[here, :]
        left[...] = left_terms(solved)
        right[...] = right_terms(solved)

        def update(i, inner):
            there = pl.ds(pl.multiple_of(i * NB, NB), NB)
            work[there, here] = jnp.zeros((NB, NB), jnp.float32)
            work[there, :] = work[there, :] - dot_tn(left[:, there], right[...])
            return inner

        lax.fori_loop(k + 1, count, update, 0)
        return carry

    lax.fori_loop(0, count, step, 0)

    def finish(k, carry):
        here = pl.ds(pl.multiple_of(k * NB, NB), NB)
        keep = lax.broadcasted_iota(jnp.int32, (NB, size), 1) <= (
            lax.broadcasted_iota(jnp.int32, (NB, size), 0) + k * NB
        )
        value = jnp.where(keep, work[here, :], 0.0)
        hi = value.astype(jnp.bfloat16)
        hi_ref[here, :] = hi
        lo_ref[here, :] = (value - hi.astype(jnp.float32)).astype(jnp.bfloat16)
        return carry

    lax.fori_loop(0, count, finish, 0)


def inverse_factor(diag):
    size = diag.shape[0]
    half = jax.ShapeDtypeStruct((size, size), jnp.bfloat16)
    return pl.pallas_call(
        factor_kernel,
        out_shape=(half, half),
        in_specs=[VMEM],
        out_specs=(VMEM, VMEM),
        scratch_shapes=[
            pltpu.VMEM((size, size), jnp.float32),
            pltpu.VMEM((NB, 2 * NB), jnp.float32),
            pltpu.VMEM((6 * NB, size), jnp.bfloat16),
            pltpu.VMEM((6 * NB, size), jnp.bfloat16),
        ],
        compiler_params=pltpu.CompilerParams(vmem_limit_bytes=40 * 2**20),
        cost_estimate=pl.CostEstimate(
            flops=2 * 6 * size**3, bytes_accessed=8 * size * size, transcendentals=0
        ),
        name="inverse_factor",
    )(diag)


def solve_rows(x, hi_ref, lo_ref):
    size = hi_ref.shape[0]
    width = 256
    parts = []
    for j in range(size // width):
        rows, upto = slice(j * width, (j + 1) * width), (j + 1) * width
        parts.append(
            dot_nt(x[:, :upto], hi_ref[rows, :upto]) + dot_nt(x[:, :upto], lo_ref[rows, :upto])
        )
    return jnp.concatenate(parts, 1).astype(jnp.bfloat16)


def apply_kernel(
    rows_b,
    index_ref,
    hi_ref,
    lo_ref,
    top_ref,
    own_ref,
    incoming_ref,
    diag_ref,
    panel_ref,
    factor_out,
    top_out,
    diag_out,
    panel_out,
    top_all,
):
    size = hi_ref.shape[0]
    local = top_out.shape[0]

    def block_of(i):
        return pl.ds(pl.multiple_of(i * rows_b, rows_b), rows_b)

    def do_top(i, carry):
        top_all[block_of(i), :] = solve_rows(top_ref[block_of(i), :], hi_ref, lo_ref)
        return carry

    def do_own(i, carry):
        factor_out[block_of(i), :] = solve_rows(own_ref[block_of(i), :], hi_ref, lo_ref)
        return carry

    lax.fori_loop(0, size // rows_b, do_top, 0)
    lax.fori_loop(0, own_ref.shape[0] // rows_b, do_own, 0)
    mine = top_all[pl.ds(pl.multiple_of(index_ref[0] * local, local), local), :]
    top_out[...] = mine
    diag_out[...] = diag_ref[...] - dot_nt(mine, top_all[...])
    panel_out[...] = panel_ref[...].astype(jnp.float32)

    def do_update(i, carry):
        solved = solve_rows(incoming_ref[block_of(i), :], hi_ref, lo_ref)
        change = dot_nt(solved, top_all[...]).astype(jnp.bfloat16)
        slot = block_of(jnp.maximum(index_ref[1 + i], 0))
        panel_out[slot, :] = panel_out[slot, :] - change.astype(jnp.float32)
        return carry

    lax.fori_loop(0, incoming_ref.shape[0] // rows_b, do_update, 0)


def apply_factor(rows_b, index, hi, lo, top, own, incoming, diag_two, panel_two):
    size = hi.shape[0]
    return pl.pallas_call(
        functools.partial(apply_kernel, rows_b),
        out_shape=(
            jax.ShapeDtypeStruct(own.shape, jnp.bfloat16),
            jax.ShapeDtypeStruct(diag_two.shape, jnp.bfloat16),
            jax.ShapeDtypeStruct(diag_two.shape, jnp.float32),
            jax.ShapeDtypeStruct(panel_two.shape, jnp.float32),
        ),
        in_specs=[pl.BlockSpec(memory_space=pltpu.SMEM)] + [VMEM] * 7,
        out_specs=(VMEM,) * 4,
        scratch_shapes=[pltpu.VMEM((size, size), jnp.bfloat16)],
        compiler_params=pltpu.CompilerParams(vmem_limit_bytes=48 * 2**20),
        cost_estimate=pl.CostEstimate(
            flops=2 * size * size * (3 * incoming.shape[0] + 3 * size),
            bytes_accessed=16 * size * size,
            transcendentals=0,
        ),
        name="apply_factor",
    )(index, hi, lo, top, own, incoming, diag_two, panel_two)


def on_device(diag_one, top_rows, panel_one, first_block, target, diag_two, panel_two):
    col_count = diag_one.shape[1]
    blocks = first_block.shape[0]
    block_rows = panel_one.shape[0] // blocks
    grid_rows = lax.axis_size("prow")
    grid_cols = lax.axis_size("pcol")
    whole_diag = lax.all_gather(diag_one, "pcol", axis=0, tiled=True)
    whole_top = lax.all_gather(top_rows, "pcol", axis=0, tiled=True)

    columns = jnp.arange(col_count, dtype=jnp.int32) // block_rows
    keep = columns[None, :] >= first_block[:, None]
    stacked = panel_one.reshape(blocks, block_rows, col_count)
    masked = jnp.where(keep[:, None, :], stacked, jnp.zeros_like(stacked))

    dest_row = target // (blocks * grid_cols)
    dest_slot = target % blocks
    routing = dest_row[None, :] == jnp.arange(grid_rows, dtype=jnp.int32)[:, None]
    send_slot = jnp.sum(jnp.where(routing, dest_slot[None, :] + 1, 0), axis=1) - 1
    outgoing = jnp.zeros((grid_rows, block_rows, col_count), jnp.bfloat16)
    for r in range(blocks):
        outgoing = jnp.where(routing[:, r, None, None], masked[r][None], outgoing)
    incoming = lax.all_to_all(outgoing, "prow", split_axis=0, concat_axis=0, tiled=True)
    incoming_slot = lax.all_to_all(send_slot, "prow", split_axis=0, concat_axis=0, tiled=True)
    index = jnp.concatenate(
        [lax.axis_index("pcol").astype(jnp.int32)[None], incoming_slot]
    )

    hi, lo = inverse_factor(whole_diag)
    panel_factor, top_own, diag_next, panel_next = apply_factor(
        block_rows,
        index,
        hi,
        lo,
        whole_top,
        masked.reshape(blocks * block_rows, col_count),
        incoming.reshape(grid_rows * block_rows, col_count),
        diag_two,
        panel_two,
    )
    return (panel_factor, top_own, diag_next, panel_next)


def solution(mesh):
    in_specs = (
        P("pcol", None),
        P("pcol", None),
        P(("prow", "pcol"), None),
        P(("prow", "pcol")),
        P(("prow", "pcol")),
        P("pcol", None),
        P(("prow", "pcol"), None),
    )
    out_specs = (
        P(("prow", "pcol"), None),
        P("pcol", None),
        P("pcol", None),
        P(("prow", "pcol"), None),
    )
    return jax.shard_map(
        on_device, mesh=mesh, in_specs=in_specs, out_specs=out_specs, check_vma=False
    )
```

```python
import functools

import jax
import jax.numpy as jnp
from jax import lax
from jax.experimental import pallas as pl
from jax.experimental.pallas import tpu as pltpu
from jax.sharding import PartitionSpec as P

NB = 128
SUB = 32
VMEM = pl.BlockSpec(memory_space=pltpu.VMEM)


def split3(x):
    hi = x.astype(jnp.bfloat16)
    rest = x - hi.astype(jnp.float32)
    mid = rest.astype(jnp.bfloat16)
    low = (rest - mid.astype(jnp.float32)).astype(jnp.bfloat16)
    return hi, mid, low


def left_terms(x):
    hi, mid, low = split3(x)
    return jnp.concatenate([hi, hi, mid, hi, low, mid], 0)


def right_terms(x):
    hi, mid, low = split3(x)
    return jnp.concatenate([hi, mid, hi, low, hi, mid], 0)


def dot_tn(left, right):
    return lax.dot_general(
        left, right, (((0,), (0,)), ((), ())), preferred_element_type=jnp.float32
    )


def dot_nt(left, right):
    return lax.dot_general(
        left, right, (((1,), (1,)), ((), ())), preferred_element_type=jnp.float32
    )


def lanes(x, column, width):
    return jnp.broadcast_to(x[:, column : column + 1], (x.shape[0], width))


def wide(x, width):
    return jnp.tile(x, (1, width // x.shape[1]))


def eliminate(rows, base):
    width = rows[0].shape[1]
    groups = len(rows)
    rows = list(rows)
    done = []
    sublane = lax.broadcasted_iota(jnp.int32, (8, width), 0)
    for q in range(groups):
        first = base + 8 * q
        cols = [lanes(rows[q], first + c, NB) for c in range(8)]
        entry = {}
        for c in range(8):
            for i in range(c, 8):
                entry[i, c] = jnp.broadcast_to(cols[c][i : i + 1, :], (8, NB))
        row = [jnp.broadcast_to(rows[q][i : i + 1, :], (8, width)) for i in range(8)]
        below = [
            [lanes(rows[p], first + c, NB) for c in range(8)] for p in range(q + 1, groups)
        ]
        scale = []
        for j in range(8):
            pivot = entry[j, j]
            inverse = 1.0 / pivot
            scale.append(lax.rsqrt(pivot))
            ratio = {c: entry[c, j] * inverse for c in range(j + 1, 8)}
            for c in range(j + 1, 8):
                for i in range(c, 8):
                    entry[i, c] = entry[i, c] - entry[i, j] * ratio[c]
                row[c] = row[c] - wide(ratio[c], width) * row[j]
            for part in below:
                for c in range(j + 1, 8):
                    part[c] = part[c] - part[j] * ratio[c]
        final = [row[i] * wide(scale[i], width) for i in range(8)]
        merged = final[0]
        for i in range(1, 8):
            merged = jnp.where(sublane == i, final[i], merged)
        done.append(merged)
        for p, part in enumerate(below):
            for c in range(8):
                rows[q + 1 + p] = rows[q + 1 + p] - wide(part[c] * scale[c], width) * final[c]
    return done


def factor_block(block):
    rows = [block[8 * i : 8 * i + 8] for i in range(NB // 8)]
    step = SUB // 8
    done = []
    for b in range(NB // SUB):
        part = eliminate(rows[b * step : (b + 1) * step], b * SUB)
        done += part
        if (b + 1) * SUB < NB:
            solved = jnp.concatenate(part, 0)
            change = dot_tn(left_terms(solved[:, (b + 1) * SUB : NB]), right_terms(solved))
            for p in range((b + 1) * step, NB // 8):
                k = p - (b + 1) * step
                rows[p] = rows[p] - change[8 * k : 8 * k + 8]
    return jnp.concatenate(done, 0)


def assemble_pieces(place_ref, mine_ref, other_ref, work):
    inner = 2
    strips, half, width = mine_ref.shape
    count = work.shape[0] // NB
    for core, ref in enumerate((mine_ref, other_ref)):
        for slot in range(strips):
            strip = (place_ref[0] ^ (slot // inner)) * inner + (place_ref[1] ^ (slot % inner))
            row = pl.multiple_of(strip * NB + (place_ref[2] ^ core) * half, half)
            for d in range(width // NB):
                column = pl.multiple_of(((strip + d) % count) * NB, NB)
                work[pl.ds(row, half), pl.ds(column, NB)] = ref[slot, :, d * NB : (d + 1) * NB]
    for i in range(count):
        for j in range(i + width // NB, count):
            here, there = slice(i * NB, (i + 1) * NB), slice(j * NB, (j + 1) * NB)
            work[here, there] = work[there, here].T


def factor_pieces_kernel(place_ref, mine_ref, other_ref, *rest):
    assemble_pieces(place_ref, mine_ref, other_ref, rest[2])
    factor_kernel(*rest)


def factor_whole_kernel(diag_ref, *rest):
    rest[2][...] = diag_ref[...]
    factor_kernel(*rest)


def factor_kernel(hi_ref, lo_ref, work, block, left, right):
    size = work.shape[0]
    count = size // NB
    same = lax.broadcasted_iota(jnp.int32, (NB, NB), 0) == lax.broadcasted_iota(
        jnp.int32, (NB, NB), 1
    )
    unit = same.astype(jnp.float32)

    def step(k, carry):
        here = pl.ds(pl.multiple_of(k * NB, NB), NB)
        block[:, :NB] = work[here, here]
        block[:, NB:] = unit
        block[...] = factor_block(block[...])
        inverse = block[:, NB:]
        solved = dot_tn(left_terms(inverse.T), right_terms(work[here, :]))
        work[here, :] = solved
        work[here, here] = inverse
        solved = work[here, :]
        left[...] = left_terms(solved)
        right[...] = right_terms(solved)

        def update(i, inner):
            there = pl.ds(pl.multiple_of(i * NB, NB), NB)
            work[there, here] = jnp.zeros((NB, NB), jnp.float32)
            work[there, :] = work[there, :] - dot_tn(left[:, there], right[...])
            return inner

        lax.fori_loop(k + 1, count, update, 0)
        return carry

    lax.fori_loop(0, count, step, 0)

    def finish(k, carry):
        here = pl.ds(pl.multiple_of(k * NB, NB), NB)
        keep = lax.broadcasted_iota(jnp.int32, (NB, size), 1) <= (
            lax.broadcasted_iota(jnp.int32, (NB, size), 0) + k * NB
        )
        value = jnp.where(keep, work[here, :], 0.0)
        hi = value.astype(jnp.bfloat16)
        hi_ref[here, :] = hi
        lo_ref[here, :] = (value - hi.astype(jnp.float32)).astype(jnp.bfloat16)
        return carry

    lax.fori_loop(0, count, finish, 0)


def inverse_factor(kernel, in_specs, size, operands):
    half = jax.ShapeDtypeStruct((size, size), jnp.bfloat16)
    return pl.pallas_call(
        kernel,
        out_shape=(half, half),
        in_specs=in_specs,
        out_specs=(VMEM, VMEM),
        scratch_shapes=[
            pltpu.VMEM((size, size), jnp.float32),
            pltpu.VMEM((NB, 2 * NB), jnp.float32),
            pltpu.VMEM((6 * NB, size), jnp.bfloat16),
            pltpu.VMEM((6 * NB, size), jnp.bfloat16),
        ],
        compiler_params=pltpu.CompilerParams(vmem_limit_bytes=40 * 2**20),
        cost_estimate=pl.CostEstimate(
            flops=2 * 6 * size**3, bytes_accessed=8 * size * size, transcendentals=0
        ),
        name="inverse_factor",
    )(*operands)


def gather_and_factor(strip):
    rows, size = strip.shape
    count = lax.axis_size("pcol")
    if rows != NB or count != 8:
        whole = lax.all_gather(strip, "pcol", axis=0, tiled=True)
        return inverse_factor(factor_whole_kernel, [VMEM], size, (whole,))
    column = lax.axis_index("pcol")
    outer, inner, core = column // 2, column % 2, lax.axis_index("prow") % 2
    reach = (count // 2 + 1) * NB
    piece = lax.dynamic_slice_in_dim(strip, core * (rows // 2), rows // 2, 0)
    piece = lax.dynamic_slice_in_dim(
        jnp.concatenate([piece, piece], 1), column * NB, reach, 1
    )
    got = [piece]
    for s in range(1, count // 2):
        got.append(
            lax.ppermute(piece, "pcol", [(i, (i // 2 ^ s) * 2 + i % 2) for i in range(count)])
        )
    both = []
    for part in got:
        both += [part, lax.ppermute(part, "pcol", [(i, i ^ 1) for i in range(count)])]
    mine = jnp.stack(both)
    other = lax.ppermute(mine, "prow", [(i, i ^ 1) for i in range(lax.axis_size("prow"))])
    place = jnp.stack([outer, inner, core]).astype(jnp.int32)
    return inverse_factor(
        factor_pieces_kernel,
        [pl.BlockSpec(memory_space=pltpu.SMEM), VMEM, VMEM],
        size,
        (place, mine, other),
    )


def solve_rows(x, hi_ref, lo_ref):
    size = hi_ref.shape[0]
    width = 256
    parts = []
    for j in range(size // width):
        rows, upto = slice(j * width, (j + 1) * width), (j + 1) * width
        parts.append(
            dot_nt(x[:, :upto], hi_ref[rows, :upto]) + dot_nt(x[:, :upto], lo_ref[rows, :upto])
        )
    return jnp.concatenate(parts, 1).astype(jnp.bfloat16)


def apply_kernel(
    rows_b,
    index_ref,
    hi_ref,
    lo_ref,
    top_ref,
    own_ref,
    incoming_ref,
    diag_ref,
    panel_ref,
    factor_out,
    top_out,
    diag_out,
    panel_out,
    top_all,
):
    size = hi_ref.shape[0]
    local = top_out.shape[0]

    def block_of(i):
        return pl.ds(pl.multiple_of(i * rows_b, rows_b), rows_b)

    def do_top(i, carry):
        top_all[block_of(i), :] = solve_rows(top_ref[block_of(i), :], hi_ref, lo_ref)
        return carry

    def do_own(i, carry):
        factor_out[block_of(i), :] = solve_rows(own_ref[block_of(i), :], hi_ref, lo_ref)
        return carry

    lax.fori_loop(0, size // rows_b, do_top, 0)
    lax.fori_loop(0, own_ref.shape[0] // rows_b, do_own, 0)
    mine = top_all[pl.ds(pl.multiple_of(index_ref[0] * local, local), local), :]
    top_out[...] = mine
    diag_out[...] = diag_ref[...] - dot_nt(mine, top_all[...])
    panel_out[...] = panel_ref[...].astype(jnp.float32)

    def do_update(i, carry):
        solved = solve_rows(incoming_ref[block_of(i), :], hi_ref, lo_ref)
        change = dot_nt(solved, top_all[...]).astype(jnp.bfloat16)
        slot = block_of(jnp.maximum(index_ref[1 + i], 0))
        panel_out[slot, :] = panel_out[slot, :] - change.astype(jnp.float32)
        return carry

    lax.fori_loop(0, incoming_ref.shape[0] // rows_b, do_update, 0)


def apply_factor(rows_b, index, hi, lo, top, own, incoming, diag_two, panel_two):
    size = hi.shape[0]
    return pl.pallas_call(
        functools.partial(apply_kernel, rows_b),
        out_shape=(
            jax.ShapeDtypeStruct(own.shape, jnp.bfloat16),
            jax.ShapeDtypeStruct(diag_two.shape, jnp.bfloat16),
            jax.ShapeDtypeStruct(diag_two.shape, jnp.float32),
            jax.ShapeDtypeStruct(panel_two.shape, jnp.float32),
        ),
        in_specs=[pl.BlockSpec(memory_space=pltpu.SMEM)] + [VMEM] * 7,
        out_specs=(VMEM,) * 4,
        scratch_shapes=[pltpu.VMEM((size, size), jnp.bfloat16)],
        compiler_params=pltpu.CompilerParams(vmem_limit_bytes=48 * 2**20),
        cost_estimate=pl.CostEstimate(
            flops=2 * size * size * (3 * incoming.shape[0] + 3 * size),
            bytes_accessed=16 * size * size,
            transcendentals=0,
        ),
        name="apply_factor",
    )(index, hi, lo, top, own, incoming, diag_two, panel_two)


def on_device(diag_one, top_rows, panel_one, first_block, target, diag_two, panel_two):
    col_count = diag_one.shape[1]
    blocks = first_block.shape[0]
    block_rows = panel_one.shape[0] // blocks
    grid_rows = lax.axis_size("prow")
    grid_cols = lax.axis_size("pcol")
    whole_top = lax.all_gather(top_rows, "pcol", axis=0, tiled=True)

    columns = jnp.arange(col_count, dtype=jnp.int32) // block_rows
    keep = columns[None, :] >= first_block[:, None]
    stacked = panel_one.reshape(blocks, block_rows, col_count)
    masked = jnp.where(keep[:, None, :], stacked, jnp.zeros_like(stacked))

    dest_row = target // (blocks * grid_cols)
    dest_slot = target % blocks
    routing = dest_row[None, :] == jnp.arange(grid_rows, dtype=jnp.int32)[:, None]
    send_slot = jnp.sum(jnp.where(routing, dest_slot[None, :] + 1, 0), axis=1) - 1
    outgoing = jnp.zeros((grid_rows, block_rows, col_count), jnp.bfloat16)
    for r in range(blocks):
        outgoing = jnp.where(routing[:, r, None, None], masked[r][None], outgoing)
    incoming = lax.all_to_all(outgoing, "prow", split_axis=0, concat_axis=0, tiled=True)
    incoming_slot = lax.all_to_all(send_slot, "prow", split_axis=0, concat_axis=0, tiled=True)
    index = jnp.concatenate(
        [lax.axis_index("pcol").astype(jnp.int32)[None], incoming_slot]
    )

    hi, lo = gather_and_factor(diag_one)
    panel_factor, top_own, diag_next, panel_next = apply_factor(
        block_rows,
        index,
        hi,
        lo,
        whole_top,
        masked.reshape(blocks * block_rows, col_count),
        incoming.reshape(grid_rows * block_rows, col_count),
        diag_two,
        panel_two,
    )
    return (panel_factor, top_own, diag_next, panel_next)


def solution(mesh):
    in_specs = (
        P("pcol", None),
        P("pcol", None),
        P(("prow", "pcol"), None),
        P(("prow", "pcol")),
        P(("prow", "pcol")),
        P("pcol", None),
        P(("prow", "pcol"), None),
    )
    out_specs = (
        P(("prow", "pcol"), None),
        P("pcol", None),
        P("pcol", None),
        P(("prow", "pcol"), None),
    )
    return jax.shard_map(
        on_device, mesh=mesh, in_specs=in_specs, out_specs=out_specs, check_vma=False
    )
```

```python
import functools

import jax
import jax.numpy as jnp
from jax import lax
from jax.experimental import pallas as pl
from jax.experimental.pallas import tpu as pltpu
from jax.sharding import PartitionSpec as P

NB = 128
SUB = 32
VMEM = pl.BlockSpec(memory_space=pltpu.VMEM)
ANY = pl.BlockSpec(memory_space=pl.ANY)
SMEM = pl.BlockSpec(memory_space=pltpu.SMEM)


def split3(x):
    hi = x.astype(jnp.bfloat16)
    rest = x - hi.astype(jnp.float32)
    mid = rest.astype(jnp.bfloat16)
    low = (rest - mid.astype(jnp.float32)).astype(jnp.bfloat16)
    return hi, mid, low


def left_terms(x):
    hi, mid, low = split3(x)
    return jnp.concatenate([hi, hi, mid], 0)


def right_terms(x):
    hi, mid, low = split3(x)
    return jnp.concatenate([hi, mid, hi], 0)


def dot_tn(left, right):
    return lax.dot_general(
        left, right, (((0,), (0,)), ((), ())), preferred_element_type=jnp.float32
    )


def dot_nt(left, right):
    return lax.dot_general(
        left, right, (((1,), (1,)), ((), ())), preferred_element_type=jnp.float32
    )


def lanes(x, column):
    return jnp.broadcast_to(x[:, column : column + 1], (8, NB))


def sublanes(x, i):
    return jnp.broadcast_to(x[i : i + 1, :], x.shape)


def wide(x, width):
    return jnp.tile(x, (1, width // x.shape[1]))


def eliminate(rows, base):
    width = rows[0].shape[1]
    groups = len(rows)
    rows = list(rows)
    done = []
    sublane = lax.broadcasted_iota(jnp.int32, (8, NB), 0)

    def columns(q):
        return [
            {p: lanes(rows[p], base + 8 * q + c) for p in range(q, groups)} for c in range(8)
        ]

    now = columns(0)
    for q in range(groups):
        later = columns(q + 1) if q + 1 < groups else []
        pivots = None
        for j in range(8):
            pivot = sublanes(now[j][q], j)
            pivots = pivot if pivots is None else jnp.where(sublane == j, pivot, pivots)
            inverse = 1.0 / pivot
            ratio = {p: now[j][p] * inverse for p in range(q, groups)}
            for c in range(j + 1, 8):
                entry = sublanes(now[j][q], c)
                for p in range(q, groups):
                    now[c][p] = now[c][p] - ratio[p] * entry
            for c in range(len(later)):
                entry = sublanes(now[j][q + 1], c)
                for p in range(q + 1, groups):
                    later[c][p] = later[c][p] - ratio[p] * entry
            row = sublanes(rows[q], j)
            if j < 7:
                below = jnp.where(sublane > j, ratio[q], 0.0)
                rows[q] = rows[q] - wide(below, width) * row
            for p in range(q + 1, groups):
                rows[p] = rows[p] - wide(ratio[p], width) * row
        done.append(rows[q] * wide(lax.rsqrt(pivots), width))
        now = later
    return done


def factor_block(block):
    rows = [block[8 * i : 8 * i + 8] for i in range(NB // 8)]
    step = SUB // 8
    done = []
    for b in range(NB // SUB):
        part = eliminate(rows[b * step : (b + 1) * step], b * SUB)
        done += part
        if (b + 1) * SUB < NB:
            solved = jnp.concatenate(part, 0)
            change = dot_tn(left_terms(solved[:, (b + 1) * SUB : NB]), right_terms(solved))
            for p in range((b + 1) * step, NB // 8):
                k = p - (b + 1) * step
                rows[p] = rows[p] - change[8 * k : 8 * k + 8]
    return jnp.concatenate(done, 0)


def assemble_pieces(place_ref, pieces, work, sems):
    half, width = pieces[0].shape
    count = work.shape[0] // NB
    column, place = place_ref[0], place_ref[1] % 2
    copies = []
    for i, ref in enumerate(pieces):
        core, crossed, turn = i // count, i // (count // 2) % 2, i % (count // 2)
        strip = column ^ (2 * turn + crossed)
        row = pl.multiple_of(strip * NB + (place ^ core) * half, half)
        for d in range(width // NB):
            lane = pl.multiple_of(((strip + d) % count) * NB, NB)
            copies.append(
                pltpu.make_async_copy(
                    ref.at[:, d * NB : (d + 1) * NB],
                    work.at[pl.ds(row, half), pl.ds(lane, NB)],
                    sems.at[len(copies)],
                )
            )
    for copy in copies:
        copy.start()
    for copy in copies:
        copy.wait()
    for i in range(count):
        for j in range(i + width // NB, count):
            here, there = slice(i * NB, (i + 1) * NB), slice(j * NB, (j + 1) * NB)
            work[here, there] = work[there, here].T


def factor_pieces_kernel(pieces, place_ref, *refs):
    *rest, sems = refs[pieces:]
    assemble_pieces(place_ref, refs[:pieces], rest[4], sems)
    factor_kernel(*rest)


def factor_whole_kernel(diag_ref, *refs):
    *rest, _ = refs
    rest[4][...] = diag_ref[...]
    factor_kernel(*rest)


def factor_kernel(own_ref, hi_ref, lo_ref, own_out, work, block, left, right):
    size = work.shape[0]
    count = size // NB
    same = lax.broadcasted_iota(jnp.int32, (NB, NB), 0) == lax.broadcasted_iota(
        jnp.int32, (NB, NB), 1
    )
    unit = same.astype(jnp.float32)

    def strip(k, to=None):
        return slice(k * NB, (k + 1 if to is None else to) * NB)

    def solve(k, inverse, columns):
        solved = dot_tn(inverse, right_terms(work[strip(k), columns]))
        work[strip(k), columns] = solved
        left[k % 2, :, columns] = left_terms(solved)
        right[k % 2, :, columns] = right_terms(solved)

    def update(i, k, columns):
        work[strip(i), columns] = work[strip(i), columns] - dot_tn(
            left[k % 2, :, strip(i)], right[k % 2, :, columns]
        )

    def rest(k, inverse, plain):
        if k + 2 < count:
            solve(k, inverse, strip(k + 2, count))
        if k:
            solve(k, inverse, strip(0, k))
        work[strip(k), strip(k)] = plain
        right[k % 2, :, strip(k)] = right_terms(plain)
        upto = (k + 1) * NB
        value = work[strip(k), :upto]
        hi = value.astype(jnp.bfloat16)
        lo = (value - hi.astype(jnp.float32)).astype(jnp.bfloat16)
        hi_ref[strip(k), :upto] = hi
        lo_ref[strip(k), :upto] = lo
        if upto < size:
            hi_ref[strip(k), upto:] = jnp.zeros((NB, size - upto), jnp.bfloat16)
            lo_ref[strip(k), upto:] = jnp.zeros((NB, size - upto), jnp.bfloat16)
        rows = own_ref[:, :upto]
        own_out[:, strip(k)] = (dot_nt(rows, hi) + dot_nt(rows, lo)).astype(jnp.bfloat16)
        for i in range(k + 1, count):
            first = i + 1 if i == k + 1 else i
            if first < count:
                update(i, k, strip(first, count))
            work[strip(i), strip(k)] = jnp.zeros((NB, NB), jnp.float32)
            update(i, k, strip(0, k + 1))

    pending = None
    for k in range(count):
        block[k % 2, :, :NB] = work[strip(k), strip(k)]
        block[k % 2, :, NB:] = unit
        block[k % 2] = factor_block(block[k % 2])
        if pending is not None:
            rest(*pending)
        plain = block[k % 2, :, NB:]
        inverse = left_terms(plain.T)
        if k + 1 < count:
            solve(k, inverse, strip(k + 1))
            update(k + 1, k, strip(k + 1))
        pending = (k, inverse, plain)
    rest(*pending)


def inverse_factor(kernel, in_specs, size, operands):
    half = jax.ShapeDtypeStruct((size, size), jnp.bfloat16)
    return pl.pallas_call(
        kernel,
        out_shape=(half, half, jax.ShapeDtypeStruct(operands[-1].shape, jnp.bfloat16)),
        in_specs=in_specs,
        out_specs=(VMEM,) * 3,
        scratch_shapes=[
            pltpu.VMEM((size, size), jnp.float32),
            pltpu.VMEM((2, NB, 2 * NB), jnp.float32),
            pltpu.VMEM((2, 3 * NB, size), jnp.bfloat16),
            pltpu.VMEM((2, 3 * NB, size), jnp.bfloat16),
            pltpu.SemaphoreType.DMA((80,)),
        ],
        compiler_params=pltpu.CompilerParams(vmem_limit_bytes=20 * 2**20),
        cost_estimate=pl.CostEstimate(
            flops=40 * size**3, bytes_accessed=8 * size * size, transcendentals=0
        ),
        name="inverse_factor",
    )(*operands)


def shifted(x, axis, s):
    return lax.ppermute(x, axis, [(i, i ^ s) for i in range(lax.axis_size(axis))])


def cut_piece(strip):
    rows, size = strip.shape
    core = lax.axis_index("prow") % 2
    piece = lax.dynamic_slice_in_dim(strip, core * (rows // 2), rows // 2, 0)
    return lax.dynamic_slice_in_dim(
        jnp.concatenate([piece, piece], 1), lax.axis_index("pcol") * rows, size // 2 + rows, 1
    )


def factor_pieces(place, size, mine, own):
    pieces = mine + [shifted(part, "prow", 1) for part in mine]
    return inverse_factor(
        functools.partial(factor_pieces_kernel, len(pieces)),
        [SMEM] + [ANY] * len(pieces) + [VMEM],
        size,
        (place, *pieces, own),
    )


def solve_rows(x, hi_ref, lo_ref):
    size = hi_ref.shape[0]
    width = 256
    parts = []
    for j in range(size // width):
        rows, upto = slice(j * width, (j + 1) * width), (j + 1) * width
        parts.append(
            dot_nt(x[:, :upto], hi_ref[rows, :upto]) + dot_nt(x[:, :upto], lo_ref[rows, :upto])
        )
    return jnp.concatenate(parts, 1).astype(jnp.bfloat16)


def top_kernel(hi_ref, lo_ref, first_ref, second_ref, out_ref):
    rows = first_ref.shape[0]
    for c, ref in enumerate((first_ref, second_ref)):
        out_ref[c * rows : (c + 1) * rows, :] = solve_rows(ref[...], hi_ref, lo_ref)


def solve_top(hi, lo, first, second):
    size = hi.shape[0]
    rows = 2 * first.shape[0]
    return pl.pallas_call(
        top_kernel,
        out_shape=jax.ShapeDtypeStruct((rows, size), jnp.bfloat16),
        in_specs=[VMEM] * 4,
        out_specs=VMEM,
        compiler_params=pltpu.CompilerParams(vmem_limit_bytes=12 * 2**20),
        cost_estimate=pl.CostEstimate(
            flops=3 * size * size * rows, bytes_accessed=8 * size * size, transcendentals=0
        ),
        name="solve_top",
    )(hi, lo, first, second)


def route_kernel(
    block_rows, grid_cols, place_ref, first_ref, target_ref, panel_ref, _, *outs
):
    own_ref, zeros_ref, *sent_refs = outs
    blocks = first_ref.shape[0]
    size = panel_ref.shape[1]
    row = place_ref[1]
    zeros_ref[...] = jnp.zeros_like(zeros_ref)
    column_block = lax.broadcasted_iota(jnp.int32, (block_rows, size), 1) // block_rows
    for r in range(blocks):
        rows = slice(r * block_rows, (r + 1) * block_rows)
        value = panel_ref[rows, :]
        own_ref[rows, :] = jnp.where(
            column_block >= first_ref[r], value, jnp.zeros_like(value)
        )
    length = block_rows + 16
    sent = []
    for ref in sent_refs:
        sent += [ref.at[i : i + length] for i in range(0, ref.shape[0], length)]
    for s, ref in enumerate(sent):
        ref[...] = jnp.zeros_like(ref)
        for r in range(blocks):
            dest_row = target_ref[r] // (blocks * grid_cols)

            @pl.when(dest_row == row ^ s)
            def _():
                ref[:block_rows, :] = own_ref[r * block_rows : (r + 1) * block_rows, :]
                ref[block_rows:, :] = jnp.full(
                    (16, size), (target_ref[r] % blocks).astype(jnp.float32)
                ).astype(jnp.bfloat16)


def route(place, first_block, target, panel, earlier):
    blocks = first_block.shape[0]
    rows, size = panel.shape
    block_rows = rows // blocks
    grid_rows, grid_cols = lax.axis_size("prow"), lax.axis_size("pcol")
    sent = (1, 1) + (2,) * (grid_rows // 2 - 1)
    own, zeros, *sent = pl.pallas_call(
        functools.partial(route_kernel, block_rows, grid_cols),
        out_shape=(
            jax.ShapeDtypeStruct(panel.shape, jnp.bfloat16),
            jax.ShapeDtypeStruct((NB // 2, size // 2 + NB), jnp.float32),
        )
        + tuple(
            jax.ShapeDtypeStruct((n * (block_rows + 16), size), jnp.bfloat16) for n in sent
        ),
        in_specs=[SMEM] * 3 + [VMEM, ANY],
        out_specs=(VMEM,) * (2 + len(sent)),
        compiler_params=pltpu.CompilerParams(vmem_limit_bytes=12 * 2**20),
        cost_estimate=pl.CostEstimate(
            flops=0, bytes_accessed=2 * (grid_rows + 4) * rows * size, transcendentals=0
        ),
        name="route_panel",
    )(place, first_block, target, panel, earlier)
    return own, zeros, sent


def hold_kernel(x_ref, _, out_ref):
    out_ref[...] = x_ref[...]


def hold(x, earlier):
    return pl.pallas_call(
        hold_kernel,
        out_shape=jax.ShapeDtypeStruct(x.shape, x.dtype),
        in_specs=[VMEM, ANY],
        out_specs=VMEM,
        compiler_params=pltpu.CompilerParams(vmem_limit_bytes=4 * 2**20),
        cost_estimate=pl.CostEstimate(
            flops=0, bytes_accessed=8 * x.size, transcendentals=0
        ),
        name="hold_piece",
    )(x, earlier)


def doubled(held, s):
    return jnp.concatenate([held, shifted(held, "pcol", s)], 0)


def update_kernel(block_rows, place_ref, hi_ref, lo_ref, mine_ref, other_ref, *refs):
    incoming = refs[:-6]
    diag_ref, panel_ref, top_out, diag_out, panel_out, top_all = refs[-6:]
    local = top_out.shape[0]
    half = local // 2
    strips = mine_ref.shape[0] // half
    bits = strips.bit_length() - 1
    column, core = place_ref[0], place_ref[1] % 2
    for c, ref in enumerate((mine_ref, other_ref)):
        for slot in range(strips):
            strip = column ^ sum(((slot >> b) & 1) << (bits - 1 - b) for b in range(bits))
            row = pl.multiple_of(strip * local + (core ^ c) * half, half)
            top_all[pl.ds(row, half), :] = ref[slot * half : (slot + 1) * half, :]
    mine = top_all[pl.ds(pl.multiple_of(column * local, local), local), :]
    top_out[...] = mine
    diag_out[...] = diag_ref[...] - dot_nt(mine, top_all[...])
    panel_out[...] = panel_ref[...].astype(jnp.float32)
    for ref in incoming:
        solved = solve_rows(ref[:block_rows, :], hi_ref, lo_ref)
        change = dot_nt(solved, top_all[...])
        slot = jnp.max(ref[block_rows : block_rows + 16, :NB].astype(jnp.float32))
        there = pl.ds(
            pl.multiple_of(slot.astype(jnp.int32) * block_rows, block_rows), block_rows
        )
        panel_out[there, :] = panel_out[there, :] - change.astype(jnp.bfloat16).astype(jnp.float32)


def apply_updates(block_rows, place, hi, lo, mine, other, incoming, diag_two, panel_two):
    size = mine.shape[1]
    return pl.pallas_call(
        functools.partial(update_kernel, block_rows),
        out_shape=(
            jax.ShapeDtypeStruct(diag_two.shape, jnp.bfloat16),
            jax.ShapeDtypeStruct(diag_two.shape, jnp.float32),
            jax.ShapeDtypeStruct(panel_two.shape, jnp.float32),
        ),
        in_specs=[SMEM] + [VMEM] * (6 + len(incoming)),
        out_specs=(VMEM,) * 3,
        scratch_shapes=[pltpu.VMEM((size, size), jnp.bfloat16)],
        compiler_params=pltpu.CompilerParams(vmem_limit_bytes=16 * 2**20),
        cost_estimate=pl.CostEstimate(
            flops=5 * size * size * block_rows * len(incoming),
            bytes_accessed=16 * size * size,
            transcendentals=0,
        ),
        name="apply_updates",
    )(place, hi, lo, mine, other, *incoming, diag_two, panel_two)


def exchange(sent):
    received, crossing = [sent[0]], [sent[1]]
    rows = sent[0].shape[0]
    for i, pair in enumerate(sent[2:]):
        pair = shifted(pair, "prow", 2 * i + 2)
        received.append(pair[:rows])
        crossing.append(pair[rows:])
    return received + [shifted(part, "prow", 1) for part in crossing]


def on_device(diag_one, top_rows, panel_one, first_block, target, diag_two, panel_two):
    local = diag_one.shape[0]
    blocks = first_block.shape[0]
    block_rows = panel_one.shape[0] // blocks

    place = jnp.stack([lax.axis_index("pcol"), lax.axis_index("prow")]).astype(jnp.int32)
    half = lax.dynamic_slice_in_dim(
        top_rows, (lax.axis_index("prow") % 2) * (local // 2), local // 2, 0
    )
    turns = [1 << b for b in reversed(range(1, lax.axis_size("pcol").bit_length() - 1))]
    held = [half]
    for s in turns:
        held.append(doubled(held[-1], s))
    own, zeros, sent = route(place, first_block, target, panel_one, held[1])
    if local == NB and lax.axis_size("pcol") == 8:
        got = [cut_piece(diag_one)]
        got += [shifted(got[0], "pcol", s) for s in (2, 4, 6)]
        got[3] = got[3] + zeros
        across = [shifted(part, "pcol", 1) for part in got]
        across[3] = hold(across[3], held[2])
        hi, lo, panel_factor = factor_pieces(place, diag_one.shape[1], got + across, own)
    else:
        whole = lax.all_gather(diag_one, "pcol", axis=0, tiled=True)
        hi, lo, panel_factor = inverse_factor(
            factor_whole_kernel, [VMEM, VMEM], whole.shape[0], (whole, own)
        )
    incoming = exchange(sent)
    top_mine = solve_top(hi, lo, held[-1], shifted(held[-1], "pcol", 1))
    top_other = shifted(top_mine, "prow", 1)
    top_own, diag_next, panel_next = apply_updates(
        block_rows, place, hi, lo, top_mine, top_other, incoming, diag_two, panel_two
    )
    return (panel_factor, top_own, diag_next, panel_next)


def solution(mesh):
    in_specs = (
        P("pcol", None),
        P("pcol", None),
        P(("prow", "pcol"), None),
        P(("prow", "pcol")),
        P(("prow", "pcol")),
        P("pcol", None),
        P(("prow", "pcol"), None),
    )
    out_specs = (
        P(("prow", "pcol"), None),
        P("pcol", None),
        P("pcol", None),
        P(("prow", "pcol"), None),
    )
    return jax.shard_map(
        on_device, mesh=mesh, in_specs=in_specs, out_specs=out_specs, check_vma=False
    )
```

```python
import functools

import jax
import jax.numpy as jnp
from jax import lax
from jax.experimental import pallas as pl
from jax.experimental.pallas import tpu as pltpu
from jax.sharding import PartitionSpec as P

NB = 128
SUB = 32
VMEM = pl.BlockSpec(memory_space=pltpu.VMEM)
ANY = pl.BlockSpec(memory_space=pl.ANY)
SMEM = pl.BlockSpec(memory_space=pltpu.SMEM)


def split2(x):
    hi = x.astype(jnp.bfloat16)
    return hi, (x - hi.astype(jnp.float32)).astype(jnp.bfloat16)


def left_terms(x):
    hi, mid = split2(x)
    return jnp.concatenate([mid, hi, hi], 0)


def right_terms(x):
    hi, mid = split2(x)
    return jnp.concatenate([hi, mid, hi], 0)


def both_terms(x):
    hi, mid = split2(x)
    return jnp.concatenate([hi, mid, hi, hi], 0)


def dot_tn(left, right):
    return lax.dot_general(
        left, right, (((0,), (0,)), ((), ())), preferred_element_type=jnp.float32
    )


def dot_nt(left, right):
    return lax.dot_general(
        left, right, (((1,), (1,)), ((), ())), preferred_element_type=jnp.float32
    )


def lanes(x, column):
    return jnp.broadcast_to(x[:, column : column + 1], (8, NB))


def sublanes(x, i):
    return jnp.broadcast_to(x[i : i + 1, :], x.shape)


def wide(x, width):
    return jnp.tile(x, (1, width // x.shape[1]))


def eliminate(rows, base):
    width = rows[0].shape[1]
    groups = len(rows)
    rows = list(rows)
    done = []
    sublane = lax.broadcasted_iota(jnp.int32, (8, NB), 0)

    def columns(q):
        return [
            {p: lanes(rows[p], base + 8 * q + c) for p in range(q, groups)} for c in range(8)
        ]

    now = columns(0)
    for q in range(groups):
        later = columns(q + 1) if q + 1 < groups else []
        pivots = None
        for j in range(8):
            pivot = sublanes(now[j][q], j)
            pivots = pivot if pivots is None else jnp.where(sublane == j, pivot, pivots)
            inverse = 1.0 / pivot
            ratio = {p: now[j][p] * inverse for p in range(q, groups)}
            for c in range(j + 1, 8):
                entry = sublanes(now[j][q], c)
                for p in range(q, groups):
                    now[c][p] = now[c][p] - ratio[p] * entry
            for c in range(len(later)):
                entry = sublanes(now[j][q + 1], c)
                for p in range(q + 1, groups):
                    later[c][p] = later[c][p] - ratio[p] * entry
            row = sublanes(rows[q], j)
            if j < 7:
                below = jnp.where(sublane > j, ratio[q], 0.0)
                rows[q] = rows[q] - wide(below, width) * row
            for p in range(q + 1, groups):
                rows[p] = rows[p] - wide(ratio[p], width) * row
        done.append(rows[q] * wide(lax.rsqrt(pivots), width))
        now = later
    return done


def factor_block(block):
    rows = [block[8 * i : 8 * i + 8] for i in range(NB // 8)]
    step = SUB // 8
    done = []
    for b in range(NB // SUB):
        part = eliminate(rows[b * step : (b + 1) * step], b * SUB)
        done += part
        if (b + 1) * SUB < NB:
            solved = jnp.concatenate(part, 0)
            change = dot_tn(left_terms(solved[:, (b + 1) * SUB : NB]), right_terms(solved))
            for p in range((b + 1) * step, NB // 8):
                k = p - (b + 1) * step
                rows[p] = rows[p] - change[8 * k : 8 * k + 8]
    return jnp.concatenate(done, 0)


def assemble_pieces(place_ref, pieces, work, sems):
    half, width = pieces[0].shape
    count = work.shape[0] // NB
    column, place = place_ref[0], place_ref[1] % 2
    copies = []
    for i, ref in enumerate(pieces):
        core, crossed, turn = i // count, i // (count // 2) % 2, i % (count // 2)
        strip = column ^ (2 * turn + crossed)
        row = pl.multiple_of(strip * NB + (place ^ core) * half, half)
        for d in range(width // NB):
            lane = pl.multiple_of(((strip + d) % count) * NB, NB)
            copies.append(
                pltpu.make_async_copy(
                    ref.at[:, d * NB : (d + 1) * NB],
                    work.at[pl.ds(row, half), pl.ds(lane, NB)],
                    sems.at[len(copies)],
                )
            )
    for copy in copies:
        copy.start()
    for copy in copies:
        copy.wait()
    for i in range(count):
        for j in range(i + width // NB, count):
            here, there = slice(i * NB, (i + 1) * NB), slice(j * NB, (j + 1) * NB)
            work[here, there] = work[there, here].T


def factor_pieces_kernel(pieces, place_ref, *refs):
    *rest, sems = refs[pieces:]
    assemble_pieces(place_ref, refs[:pieces], rest[2], sems)
    factor_kernel(*rest)


def factor_whole_kernel(diag_ref, *refs):
    *rest, _ = refs
    rest[2][...] = diag_ref[...]
    factor_kernel(*rest)


def factor_kernel(hi_ref, lo_ref, work, block, terms):
    size = work.shape[0]
    count = size // NB
    same = lax.broadcasted_iota(jnp.int32, (NB, NB), 0) == lax.broadcasted_iota(
        jnp.int32, (NB, NB), 1
    )
    unit = same.astype(jnp.float32)

    def strip(k, to=None):
        return slice(k * NB, (k + 1 if to is None else to) * NB)

    def solve(k, inverse, columns):
        solved = dot_tn(inverse, right_terms(work[strip(k), columns]))
        work[strip(k), columns] = solved
        terms[k % 2, :, columns] = both_terms(solved)

    def update(i, k, columns):
        work[strip(i), columns] = work[strip(i), columns] - dot_tn(
            terms[k % 2, NB:, strip(i)], terms[k % 2, : 3 * NB, columns]
        )

    def rest(k, inverse, plain):
        if k + 2 < count:
            solve(k, inverse, strip(k + 2, count))
        if k:
            solve(k, inverse, strip(0, k))
        work[strip(k), strip(k)] = plain
        terms[k % 2, :, strip(k)] = both_terms(plain)
        upto = (k + 1) * NB
        value = work[strip(k), :upto]
        hi = value.astype(jnp.bfloat16)
        lo = (value - hi.astype(jnp.float32)).astype(jnp.bfloat16)
        hi_ref[strip(k), :upto] = hi
        lo_ref[strip(k), :upto] = lo
        if upto < size:
            hi_ref[strip(k), upto:] = jnp.zeros((NB, size - upto), jnp.bfloat16)
            lo_ref[strip(k), upto:] = jnp.zeros((NB, size - upto), jnp.bfloat16)
        for i in range(k + 1, count):
            first = i + 1 if i == k + 1 else i
            if first < count:
                update(i, k, strip(first, count))
            work[strip(i), strip(k)] = jnp.zeros((NB, NB), jnp.float32)
            update(i, k, strip(0, k + 1))

    pending = None
    for k in range(count):
        block[k % 2, :, :NB] = work[strip(k), strip(k)]
        block[k % 2, :, NB:] = unit
        block[k % 2] = factor_block(block[k % 2])
        if pending is not None:
            rest(*pending)
        plain = block[k % 2, :, NB:]
        inverse = left_terms(plain.T)
        if k + 1 < count:
            solve(k, inverse, strip(k + 1))
            update(k + 1, k, strip(k + 1))
        pending = (k, inverse, plain)
    rest(*pending)


def inverse_factor(kernel, in_specs, size, operands):
    half = jax.ShapeDtypeStruct((size, size), jnp.bfloat16)
    return pl.pallas_call(
        kernel,
        out_shape=(half, half),
        in_specs=in_specs,
        out_specs=(VMEM,) * 2,
        scratch_shapes=[
            pltpu.VMEM((size, size), jnp.float32),
            pltpu.VMEM((2, NB, 2 * NB), jnp.float32),
            pltpu.VMEM((2, 4 * NB, size), jnp.bfloat16),
            pltpu.SemaphoreType.DMA((80,)),
        ],
        compiler_params=pltpu.CompilerParams(vmem_limit_bytes=20 * 2**20),
        cost_estimate=pl.CostEstimate(
            flops=40 * size**3, bytes_accessed=8 * size * size, transcendentals=0
        ),
        name="inverse_factor",
    )(*operands)


def shifted(x, axis, s):
    return lax.ppermute(x, axis, [(i, i ^ s) for i in range(lax.axis_size(axis))])


def cut_piece(strip):
    rows, size = strip.shape
    core = lax.axis_index("prow") % 2
    piece = lax.dynamic_slice_in_dim(strip, core * (rows // 2), rows // 2, 0)
    return lax.dynamic_slice_in_dim(
        jnp.concatenate([piece, piece], 1), lax.axis_index("pcol") * rows, size // 2 + rows, 1
    )


def factor_pieces(place, size, mine):
    pieces = mine + [shifted(part, "prow", 1) for part in mine]
    return inverse_factor(
        functools.partial(factor_pieces_kernel, len(pieces)),
        [SMEM] + [ANY] * len(pieces),
        size,
        (place, *pieces),
    )


def solve_rows(x, hi_ref, lo_ref, out_ref):
    size = hi_ref.shape[0]
    width = 256
    for j in range(size // width):
        rows, upto = slice(j * width, (j + 1) * width), (j + 1) * width
        out_ref[:, rows] = (
            dot_nt(x[:, :upto], hi_ref[rows, :upto]) + dot_nt(x[:, :upto], lo_ref[rows, :upto])
        ).astype(jnp.bfloat16)


def solve_kernel(hi_ref, lo_ref, x_ref, out_ref):
    solve_rows(x_ref, hi_ref, lo_ref, out_ref)


def solve(hi, lo, x, name):
    size = hi.shape[0]
    return pl.pallas_call(
        solve_kernel,
        out_shape=jax.ShapeDtypeStruct(x.shape, jnp.bfloat16),
        in_specs=[VMEM] * 3,
        out_specs=VMEM,
        compiler_params=pltpu.CompilerParams(vmem_limit_bytes=12 * 2**20),
        cost_estimate=pl.CostEstimate(
            flops=3 * size * x.size, bytes_accessed=8 * size * size, transcendentals=0
        ),
        name=name,
    )(hi, lo, x)


def route_kernel(
    block_rows, grid_cols, place_ref, first_ref, target_ref, panel_ref, _, *outs
):
    own_ref, zeros_ref, *sent_refs = outs
    blocks = first_ref.shape[0]
    size = panel_ref.shape[1]
    row = place_ref[1]
    zeros_ref[...] = jnp.zeros_like(zeros_ref)
    column_block = lax.broadcasted_iota(jnp.int32, (block_rows, size), 1) // block_rows
    for r in range(blocks):
        rows = slice(r * block_rows, (r + 1) * block_rows)
        value = panel_ref[rows, :]
        own_ref[rows, :] = jnp.where(
            column_block >= first_ref[r], value, jnp.zeros_like(value)
        )
    length = block_rows + 16
    sent = []
    for ref in sent_refs:
        sent += [ref.at[i : i + length] for i in range(0, ref.shape[0], length)]
    for s, ref in enumerate(sent):
        ref[...] = jnp.zeros_like(ref)
        for r in range(blocks):
            dest_row = target_ref[r] // (blocks * grid_cols)

            @pl.when(dest_row == row ^ s)
            def _():
                ref[:block_rows, :] = own_ref[r * block_rows : (r + 1) * block_rows, :]
                ref[block_rows:, :] = jnp.full(
                    (16, size), (target_ref[r] % blocks).astype(jnp.float32)
                ).astype(jnp.bfloat16)


def route(place, first_block, target, panel, earlier):
    blocks = first_block.shape[0]
    rows, size = panel.shape
    block_rows = rows // blocks
    grid_rows, grid_cols = lax.axis_size("prow"), lax.axis_size("pcol")
    sent = (1, 1) + (2,) * (grid_rows // 2 - 1)
    own, zeros, *sent = pl.pallas_call(
        functools.partial(route_kernel, block_rows, grid_cols),
        out_shape=(
            jax.ShapeDtypeStruct(panel.shape, jnp.bfloat16),
            jax.ShapeDtypeStruct((NB // 2, size // 2 + NB), jnp.float32),
        )
        + tuple(
            jax.ShapeDtypeStruct((n * (block_rows + 16), size), jnp.bfloat16) for n in sent
        ),
        in_specs=[SMEM] * 3 + [VMEM] * 2,
        out_specs=(VMEM,) * (2 + len(sent)),
        compiler_params=pltpu.CompilerParams(vmem_limit_bytes=12 * 2**20),
        cost_estimate=pl.CostEstimate(
            flops=0, bytes_accessed=2 * (grid_rows + 4) * rows * size, transcendentals=0
        ),
        name="route_panel",
    )(place, first_block, target, panel, earlier)
    return own, zeros, sent


def hold_kernel(x_ref, _, out_ref):
    out_ref[...] = x_ref[...]


def hold(x, earlier):
    return pl.pallas_call(
        hold_kernel,
        out_shape=jax.ShapeDtypeStruct(x.shape, x.dtype),
        in_specs=[VMEM, VMEM],
        out_specs=VMEM,
        compiler_params=pltpu.CompilerParams(vmem_limit_bytes=4 * 2**20),
        cost_estimate=pl.CostEstimate(
            flops=0, bytes_accessed=8 * x.size, transcendentals=0
        ),
        name="hold_piece",
    )(x, earlier)


def doubled(held, s):
    return jnp.concatenate([held, shifted(held, "pcol", s)], 0)


def update_kernel(block_rows, place_ref, hi_ref, lo_ref, mine_ref, other_ref, *refs):
    incoming = refs[:-8]
    diag_ref, panel_ref, top_out, diag_out, panel_out, top_all, received, solved = refs[-8:]
    for i, ref in enumerate(incoming):
        received[i * block_rows : (i + 1) * block_rows, :] = ref[:block_rows, :]
    solve_rows(received, hi_ref, lo_ref, solved)
    local = top_out.shape[0]
    half = local // 2
    strips = mine_ref.shape[0] // half
    column, core = place_ref[0], place_ref[1] % 2
    for c, ref in enumerate((mine_ref, other_ref)):
        for slot in range(strips):
            row = pl.multiple_of((column ^ slot) * local + (core ^ c) * half, half)
            top_all[pl.ds(row, half), :] = ref[slot * half : (slot + 1) * half, :]
    mine = top_all[pl.ds(pl.multiple_of(column * local, local), local), :]
    top_out[...] = mine
    diag_out[...] = diag_ref[...] - dot_nt(mine, top_all[...])
    panel_out[...] = panel_ref[...].astype(jnp.float32)
    slots = [
        jnp.max(ref[block_rows : block_rows + 16, :NB].astype(jnp.float32)).astype(jnp.int32)
        for ref in incoming
    ]
    width = 256
    for j in range(0, top_all.shape[0], width):
        columns = slice(j, j + width)
        change = dot_nt(solved[...], top_all[columns, :]).astype(jnp.bfloat16).astype(jnp.float32)
        for i, slot in enumerate(slots):
            there = pl.ds(pl.multiple_of(slot * block_rows, block_rows), block_rows)
            panel_out[there, columns] = (
                panel_out[there, columns] - change[i * block_rows : (i + 1) * block_rows]
            )


def apply_updates(block_rows, place, hi, lo, mine, other, incoming, diag_two, panel_two):
    size = mine.shape[1]
    return pl.pallas_call(
        functools.partial(update_kernel, block_rows),
        out_shape=(
            jax.ShapeDtypeStruct(diag_two.shape, jnp.bfloat16),
            jax.ShapeDtypeStruct(diag_two.shape, jnp.float32),
            jax.ShapeDtypeStruct(panel_two.shape, jnp.float32),
        ),
        in_specs=[SMEM] + [VMEM] * (6 + len(incoming)),
        out_specs=(VMEM,) * 3,
        scratch_shapes=[
            pltpu.VMEM((size, size), jnp.bfloat16),
            pltpu.VMEM((block_rows * len(incoming), size), jnp.bfloat16),
            pltpu.VMEM((block_rows * len(incoming), size), jnp.bfloat16),
        ],
        compiler_params=pltpu.CompilerParams(vmem_limit_bytes=24 * 2**20),
        cost_estimate=pl.CostEstimate(
            flops=5 * size * size * block_rows * len(incoming),
            bytes_accessed=16 * size * size,
            transcendentals=0,
        ),
        name="apply_updates",
    )(place, hi, lo, mine, other, *incoming, diag_two, panel_two)


def exchange(sent):
    received, crossing = [sent[0]], [sent[1]]
    rows = sent[0].shape[0]
    for i, pair in enumerate(sent[2:]):
        pair = shifted(pair, "prow", 2 * i + 2)
        received.append(pair[:rows])
        crossing.append(pair[rows:])
    return received + [shifted(part, "prow", 1) for part in crossing]


def on_device(diag_one, top_rows, panel_one, first_block, target, diag_two, panel_two):
    local = diag_one.shape[0]
    blocks = first_block.shape[0]
    block_rows = panel_one.shape[0] // blocks

    place = jnp.stack([lax.axis_index("pcol"), lax.axis_index("prow")]).astype(jnp.int32)
    half = lax.dynamic_slice_in_dim(
        top_rows, (lax.axis_index("prow") % 2) * (local // 2), local // 2, 0
    )
    held = [half]
    while 2 * len(held[-1]) < len(half) * lax.axis_size("pcol"):
        held.append(doubled(held[-1], len(held[-1]) // len(half)))
    own, zeros, sent = route(place, first_block, target, panel_one, held[1])
    if local == NB and lax.axis_size("pcol") == 8:
        got = [cut_piece(diag_one)]
        got += [shifted(got[0], "pcol", s) for s in (2, 4)]
        got.append(shifted(got[2], "pcol", 2) + zeros)
        across = [shifted(part, "pcol", 1) for part in got]
        across[3] = hold(across[3], held[2])
        hi, lo = factor_pieces(place, diag_one.shape[1], got + across)
    else:
        whole = lax.all_gather(diag_one, "pcol", axis=0, tiled=True)
        hi, lo = inverse_factor(factor_whole_kernel, [VMEM], whole.shape[0], (whole,))
    incoming = exchange(sent)
    top_mine = solve(hi, lo, doubled(held[-1], lax.axis_size("pcol") // 2), "solve_top")
    top_other = shifted(top_mine, "prow", 1)
    panel_factor = solve(hi, lo, own, "solve_own")
    top_own, diag_next, panel_next = apply_updates(
        block_rows, place, hi, lo, top_mine, top_other, incoming, diag_two, panel_two
    )
    return (panel_factor, top_own, diag_next, panel_next)


def solution(mesh):
    in_specs = (
        P("pcol", None),
        P("pcol", None),
        P(("prow", "pcol"), None),
        P(("prow", "pcol")),
        P(("prow", "pcol")),
        P("pcol", None),
        P(("prow", "pcol"), None),
    )
    out_specs = (
        P(("prow", "pcol"), None),
        P("pcol", None),
        P("pcol", None),
        P(("prow", "pcol"), None),
    )
    return jax.shard_map(
        on_device, mesh=mesh, in_specs=in_specs, out_specs=out_specs, check_vma=False
    )
```

```python
import functools

import jax
import jax.numpy as jnp
from jax import lax
from jax.experimental import pallas as pl
from jax.experimental.pallas import tpu as pltpu
from jax.sharding import PartitionSpec as P

NB = 128
SUB = 32
VMEM = pl.BlockSpec(memory_space=pltpu.VMEM)
ANY = pl.BlockSpec(memory_space=pl.ANY)
SMEM = pl.BlockSpec(memory_space=pltpu.SMEM)


def split2(x):
    hi = x.astype(jnp.bfloat16)
    return hi, (x - hi.astype(jnp.float32)).astype(jnp.bfloat16)


def left_terms(x):
    hi, mid = split2(x)
    return jnp.concatenate([mid, hi, hi], 0)


def right_terms(x):
    hi, mid = split2(x)
    return jnp.concatenate([hi, mid, hi], 0)


def both_terms(x):
    hi, mid = split2(x)
    return jnp.concatenate([hi, mid, hi, hi], 0)


def dot_tn(left, right):
    return lax.dot_general(
        left, right, (((0,), (0,)), ((), ())), preferred_element_type=jnp.float32
    )


def dot_nt(left, right):
    return lax.dot_general(
        left, right, (((1,), (1,)), ((), ())), preferred_element_type=jnp.float32
    )


def lanes(x, column):
    return jnp.broadcast_to(x[:, column : column + 1], (8, NB))


def sublanes(x, i):
    return jnp.broadcast_to(x[i : i + 1, :], x.shape)


def wide(x, width):
    return jnp.tile(x, (1, width // x.shape[1]))


def eliminate(rows, base):
    width = rows[0].shape[1]
    groups = len(rows)
    rows = list(rows)
    done = []
    sublane = lax.broadcasted_iota(jnp.int32, (8, NB), 0)

    def columns(q):
        return [
            {p: lanes(rows[p], base + 8 * q + c) for p in range(q, groups)} for c in range(8)
        ]

    now = columns(0)
    for q in range(groups):
        later = columns(q + 1) if q + 1 < groups else []
        pivots = None
        for j in range(8):
            pivot = sublanes(now[j][q], j)
            pivots = pivot if pivots is None else jnp.where(sublane == j, pivot, pivots)
            inverse = 1.0 / pivot
            ratio = {p: now[j][p] * inverse for p in range(q, groups)}
            for c in range(j + 1, 8):
                entry = sublanes(now[j][q], c)
                for p in range(q, groups):
                    now[c][p] = now[c][p] - ratio[p] * entry
            for c in range(len(later)):
                entry = sublanes(now[j][q + 1], c)
                for p in range(q + 1, groups):
                    later[c][p] = later[c][p] - ratio[p] * entry
            row = sublanes(rows[q], j)
            if j < 7:
                below = jnp.where(sublane > j, ratio[q], 0.0)
                rows[q] = rows[q] - wide(below, width) * row
            for p in range(q + 1, groups):
                rows[p] = rows[p] - wide(ratio[p], width) * row
        done.append(rows[q] * wide(lax.rsqrt(pivots), width))
        now = later
    return done


def factor_block(block):
    rows = [block[8 * i : 8 * i + 8] for i in range(NB // 8)]
    step = SUB // 8
    done = []
    for b in range(NB // SUB):
        part = eliminate(rows[b * step : (b + 1) * step], b * SUB)
        done += part
        if (b + 1) * SUB < NB:
            solved = jnp.concatenate(part, 0)
            change = dot_tn(left_terms(solved[:, (b + 1) * SUB : NB]), right_terms(solved))
            for p in range((b + 1) * step, NB // 8):
                k = p - (b + 1) * step
                rows[p] = rows[p] - change[8 * k : 8 * k + 8]
    return jnp.concatenate(done, 0)


def assemble_pieces(place_ref, pieces, work, sems):
    half, width = pieces[0].shape
    count = work.shape[0] // NB
    column, place = place_ref[0], place_ref[1] % 2
    copies = []
    for i, ref in enumerate(pieces):
        core, crossed, turn = i // count, i // (count // 2) % 2, i % (count // 2)
        strip = column ^ (2 * turn + crossed)
        row = pl.multiple_of(strip * NB + (place ^ core) * half, half)
        for d in range(width // NB):
            lane = pl.multiple_of(((strip + d) % count) * NB, NB)
            copies.append(
                pltpu.make_async_copy(
                    ref.at[:, d * NB : (d + 1) * NB],
                    work.at[pl.ds(row, half), pl.ds(lane, NB)],
                    sems.at[len(copies)],
                )
            )
    for copy in copies:
        copy.start()
    for copy in copies:
        copy.wait()
    for i in range(count):
        for j in range(i + width // NB, count):
            here, there = slice(i * NB, (i + 1) * NB), slice(j * NB, (j + 1) * NB)
            work[here, there] = work[there, here].T


def factor_pieces_kernel(pieces, place_ref, *refs):
    *rest, sems = refs[pieces:]
    assemble_pieces(place_ref, refs[:pieces], rest[2], sems)
    factor_kernel(*rest)


def factor_whole_kernel(diag_ref, *refs):
    *rest, _ = refs
    rest[2][...] = diag_ref[...]
    factor_kernel(*rest)


def factor_kernel(hi_ref, lo_ref, work, block, terms):
    size = work.shape[0]
    count = size // NB
    same = lax.broadcasted_iota(jnp.int32, (NB, NB), 0) == lax.broadcasted_iota(
        jnp.int32, (NB, NB), 1
    )
    unit = same.astype(jnp.float32)

    def strip(k, to=None):
        return slice(k * NB, (k + 1 if to is None else to) * NB)

    def solve(k, inverse, columns):
        solved = dot_tn(inverse, right_terms(work[strip(k), columns]))
        work[strip(k), columns] = solved
        if k + 1 < count:
            terms[k % 2, :, columns] = both_terms(solved)

    def update(i, k, columns):
        work[strip(i), columns] = work[strip(i), columns] - dot_tn(
            terms[k % 2, NB:, strip(i)], terms[k % 2, : 3 * NB, columns]
        )

    def rest(k, inverse, plain):
        if k + 2 < count:
            solve(k, inverse, strip(k + 2, count))
        if k:
            solve(k, inverse, strip(0, k))
        work[strip(k), strip(k)] = plain
        if k + 1 < count:
            terms[k % 2, :, strip(k)] = both_terms(plain)
        upto = (k + 1) * NB
        value = work[strip(k), :upto]
        hi = value.astype(jnp.bfloat16)
        lo = (value - hi.astype(jnp.float32)).astype(jnp.bfloat16)
        hi_ref[strip(k), :upto] = hi
        lo_ref[strip(k), :upto] = lo
        if upto < size:
            hi_ref[strip(k), upto:] = jnp.zeros((NB, size - upto), jnp.bfloat16)
            lo_ref[strip(k), upto:] = jnp.zeros((NB, size - upto), jnp.bfloat16)
        for i in range(k + 1, count):
            first = i + 1 if i == k + 1 else i
            if first < count:
                update(i, k, strip(first, count))
            work[strip(i), strip(k)] = jnp.zeros((NB, NB), jnp.float32)
            update(i, k, strip(0, k + 1))

    pending = None
    for k in range(count):
        block[k % 2, :, :NB] = work[strip(k), strip(k)]
        block[k % 2, :, NB:] = unit
        block[k % 2] = factor_block(block[k % 2])
        if pending is not None:
            rest(*pending)
        plain = block[k % 2, :, NB:]
        inverse = left_terms(plain.T)
        if k + 1 < count:
            solve(k, inverse, strip(k + 1))
            update(k + 1, k, strip(k + 1))
        pending = (k, inverse, plain)
    rest(*pending)


def inverse_factor(kernel, in_specs, size, operands):
    half = jax.ShapeDtypeStruct((size, size), jnp.bfloat16)
    return pl.pallas_call(
        kernel,
        out_shape=(half, half),
        in_specs=in_specs,
        out_specs=(VMEM,) * 2,
        scratch_shapes=[
            pltpu.VMEM((size, size), jnp.float32),
            pltpu.VMEM((2, NB, 2 * NB), jnp.float32),
            pltpu.VMEM((2, 4 * NB, size), jnp.bfloat16),
            pltpu.SemaphoreType.DMA((80,)),
        ],
        compiler_params=pltpu.CompilerParams(vmem_limit_bytes=20 * 2**20),
        cost_estimate=pl.CostEstimate(
            flops=40 * size**3, bytes_accessed=8 * size * size, transcendentals=0
        ),
        name="inverse_factor",
    )(*operands)


def shifted(x, axis, s):
    return lax.ppermute(x, axis, [(i, i ^ s) for i in range(lax.axis_size(axis))])


def cut_piece(strip):
    rows, size = strip.shape
    core = lax.axis_index("prow") % 2
    piece = lax.dynamic_slice_in_dim(strip, core * (rows // 2), rows // 2, 0)
    return lax.dynamic_slice_in_dim(
        jnp.concatenate([piece, piece], 1), lax.axis_index("pcol") * rows, size // 2 + rows, 1
    )


def factor_pieces(place, size, mine):
    pieces = mine + [shifted(part, "prow", 1) for part in mine]
    return inverse_factor(
        functools.partial(factor_pieces_kernel, len(pieces)),
        [SMEM] + [ANY] * len(pieces),
        size,
        (place, *pieces),
    )


def solve_rows(x, hi_ref, lo_ref, out_ref):
    size = hi_ref.shape[0]
    width = 256
    for j in range(size // width):
        rows, upto = slice(j * width, (j + 1) * width), (j + 1) * width
        out_ref[:, rows] = (
            dot_nt(x[:, :upto], hi_ref[rows, :upto]) + dot_nt(x[:, :upto], lo_ref[rows, :upto])
        ).astype(jnp.bfloat16)


def solve_kernel(hi_ref, lo_ref, x_ref, out_ref):
    solve_rows(x_ref, hi_ref, lo_ref, out_ref)


def solve(hi, lo, x, name):
    size = hi.shape[0]
    return pl.pallas_call(
        solve_kernel,
        out_shape=jax.ShapeDtypeStruct(x.shape, jnp.bfloat16),
        in_specs=[VMEM] * 3,
        out_specs=VMEM,
        compiler_params=pltpu.CompilerParams(vmem_limit_bytes=12 * 2**20),
        cost_estimate=pl.CostEstimate(
            flops=3 * size * x.size, bytes_accessed=8 * size * size, transcendentals=0
        ),
        name=name,
    )(hi, lo, x)


def route_kernel(
    block_rows, grid_cols, place_ref, first_ref, target_ref, panel_ref, _, *outs
):
    own_ref, zeros_ref, *sent_refs = outs
    blocks = first_ref.shape[0]
    size = panel_ref.shape[1]
    row = place_ref[1]
    zeros_ref[...] = jnp.zeros_like(zeros_ref)
    column_block = lax.broadcasted_iota(jnp.int32, (block_rows, size), 1) // block_rows
    for r in range(blocks):
        rows = slice(r * block_rows, (r + 1) * block_rows)
        value = panel_ref[rows, :]
        own_ref[rows, :] = jnp.where(
            column_block >= first_ref[r], value, jnp.zeros_like(value)
        )
    length = block_rows + 16
    sent = []
    for ref in sent_refs:
        sent += [ref.at[i : i + length] for i in range(0, ref.shape[0], length)]
    for s, ref in enumerate(sent):
        ref[...] = jnp.zeros_like(ref)
        for r in range(blocks):
            dest_row = target_ref[r] // (blocks * grid_cols)

            @pl.when(dest_row == row ^ s)
            def _():
                ref[:block_rows, :] = own_ref[r * block_rows : (r + 1) * block_rows, :]
                ref[block_rows:, :] = jnp.full(
                    (16, size), (target_ref[r] % blocks).astype(jnp.float32)
                ).astype(jnp.bfloat16)


def route(place, first_block, target, panel, earlier):
    blocks = first_block.shape[0]
    rows, size = panel.shape
    block_rows = rows // blocks
    grid_rows, grid_cols = lax.axis_size("prow"), lax.axis_size("pcol")
    sent = (1, 1) + (2,) * (grid_rows // 2 - 1)
    own, zeros, *sent = pl.pallas_call(
        functools.partial(route_kernel, block_rows, grid_cols),
        out_shape=(
            jax.ShapeDtypeStruct(panel.shape, jnp.bfloat16),
            jax.ShapeDtypeStruct((NB // 2, size // 2 + NB), jnp.float32),
        )
        + tuple(
            jax.ShapeDtypeStruct((n * (block_rows + 16), size), jnp.bfloat16) for n in sent
        ),
        in_specs=[SMEM] * 3 + [VMEM] * 2,
        out_specs=(VMEM,) * (2 + len(sent)),
        compiler_params=pltpu.CompilerParams(vmem_limit_bytes=12 * 2**20),
        cost_estimate=pl.CostEstimate(
            flops=0, bytes_accessed=2 * (grid_rows + 4) * rows * size, transcendentals=0
        ),
        name="route_panel",
    )(place, first_block, target, panel, earlier)
    return own, zeros, sent


def hold_kernel(x_ref, _, out_ref):
    out_ref[...] = x_ref[...]


def hold(x, earlier):
    return pl.pallas_call(
        hold_kernel,
        out_shape=jax.ShapeDtypeStruct(x.shape, x.dtype),
        in_specs=[VMEM, VMEM],
        out_specs=VMEM,
        compiler_params=pltpu.CompilerParams(vmem_limit_bytes=4 * 2**20),
        cost_estimate=pl.CostEstimate(
            flops=0, bytes_accessed=8 * x.size, transcendentals=0
        ),
        name="hold_piece",
    )(x, earlier)


def doubled(held, s):
    return jnp.concatenate([held, shifted(held, "pcol", s)], 0)


def update_kernel(block_rows, place_ref, hi_ref, lo_ref, mine_ref, other_ref, *refs):
    incoming = refs[:-8]
    diag_ref, panel_ref, top_out, diag_out, panel_out, top_all, received, solved = refs[-8:]
    for i, ref in enumerate(incoming):
        received[i * block_rows : (i + 1) * block_rows, :] = ref[:block_rows, :]
    solve_rows(received, hi_ref, lo_ref, solved)
    local = top_out.shape[0]
    half = local // 2
    strips = mine_ref.shape[0] // half
    column, core = place_ref[0], place_ref[1] % 2
    for c, ref in enumerate((mine_ref, other_ref)):
        for slot in range(strips):
            row = pl.multiple_of((column ^ slot) * local + (core ^ c) * half, half)
            top_all[pl.ds(row, half), :] = ref[slot * half : (slot + 1) * half, :]
    mine = top_all[pl.ds(pl.multiple_of(column * local, local), local), :]
    top_out[...] = mine
    diag_out[...] = diag_ref[...] - dot_nt(mine, top_all[...])
    panel_out[...] = panel_ref[...].astype(jnp.float32)
    slots = [
        jnp.max(ref[block_rows : block_rows + 16, :NB].astype(jnp.float32)).astype(jnp.int32)
        for ref in incoming
    ]
    width = 256
    for j in range(0, top_all.shape[0], width):
        columns = slice(j, j + width)
        change = dot_nt(solved[...], top_all[columns, :]).astype(jnp.bfloat16).astype(jnp.float32)
        for i, slot in enumerate(slots):
            there = pl.ds(pl.multiple_of(slot * block_rows, block_rows), block_rows)
            panel_out[there, columns] = (
                panel_out[there, columns] - change[i * block_rows : (i + 1) * block_rows]
            )


def apply_updates(block_rows, place, hi, lo, mine, other, incoming, diag_two, panel_two):
    size = mine.shape[1]
    return pl.pallas_call(
        functools.partial(update_kernel, block_rows),
        out_shape=(
            jax.ShapeDtypeStruct(diag_two.shape, jnp.bfloat16),
            jax.ShapeDtypeStruct(diag_two.shape, jnp.float32),
            jax.ShapeDtypeStruct(panel_two.shape, jnp.float32),
        ),
        in_specs=[SMEM] + [VMEM] * (6 + len(incoming)),
        out_specs=(VMEM,) * 3,
        scratch_shapes=[
            pltpu.VMEM((size, size), jnp.bfloat16),
            pltpu.VMEM((block_rows * len(incoming), size), jnp.bfloat16),
            pltpu.VMEM((block_rows * len(incoming), size), jnp.bfloat16),
        ],
        compiler_params=pltpu.CompilerParams(vmem_limit_bytes=24 * 2**20),
        cost_estimate=pl.CostEstimate(
            flops=5 * size * size * block_rows * len(incoming),
            bytes_accessed=16 * size * size,
            transcendentals=0,
        ),
        name="apply_updates",
    )(place, hi, lo, mine, other, *incoming, diag_two, panel_two)


def exchange(sent):
    received, crossing = [sent[0]], [sent[1]]
    rows = sent[0].shape[0]
    for i, pair in enumerate(sent[2:]):
        pair = shifted(pair, "prow", 2 * i + 2)
        received.append(pair[:rows])
        crossing.append(pair[rows:])
    return received + [shifted(part, "prow", 1) for part in crossing]


def on_device(diag_one, top_rows, panel_one, first_block, target, diag_two, panel_two):
    local = diag_one.shape[0]
    blocks = first_block.shape[0]
    block_rows = panel_one.shape[0] // blocks

    place = jnp.stack([lax.axis_index("pcol"), lax.axis_index("prow")]).astype(jnp.int32)
    half = lax.dynamic_slice_in_dim(
        top_rows, (lax.axis_index("prow") % 2) * (local // 2), local // 2, 0
    )
    held = [half]
    while 2 * len(held[-1]) < len(half) * lax.axis_size("pcol"):
        held.append(doubled(held[-1], len(held[-1]) // len(half)))
    own, zeros, sent = route(place, first_block, target, panel_one, held[1])
    if local == NB and lax.axis_size("pcol") == 8:
        got = [cut_piece(diag_one)]
        got += [shifted(got[0], "pcol", s) for s in (2, 4)]
        got.append(shifted(got[2], "pcol", 2) + zeros)
        across = [shifted(part, "pcol", 1) for part in got]
        across[3] = hold(across[3], held[2])
        hi, lo = factor_pieces(place, diag_one.shape[1], got + across)
    else:
        whole = lax.all_gather(diag_one, "pcol", axis=0, tiled=True)
        hi, lo = inverse_factor(factor_whole_kernel, [VMEM], whole.shape[0], (whole,))
    incoming = exchange(sent)
    top_mine = solve(hi, lo, doubled(held[-1], lax.axis_size("pcol") // 2), "solve_top")
    top_other = shifted(top_mine, "prow", 1)
    panel_factor = solve(hi, lo, own, "solve_own")
    top_own, diag_next, panel_next = apply_updates(
        block_rows, place, hi, lo, top_mine, top_other, incoming, diag_two, panel_two
    )
    return (panel_factor, top_own, diag_next, panel_next)


def solution(mesh):
    in_specs = (
        P("pcol", None),
        P("pcol", None),
        P(("prow", "pcol"), None),
        P(("prow", "pcol")),
        P(("prow", "pcol")),
        P("pcol", None),
        P(("prow", "pcol"), None),
    )
    out_specs = (
        P(("prow", "pcol"), None),
        P("pcol", None),
        P("pcol", None),
        P(("prow", "pcol"), None),
    )
    return jax.shard_map(
        on_device, mesh=mesh, in_specs=in_specs, out_specs=out_specs, check_vma=False
    )
```
